32 devices in a mesh: groups: 2 (over y), attn: 8 (over z, core), ffn: 2 (over x).
Axes of the slice: x: 2, y: 2, z: 4, core: 2. Of those that a mesh axis runs over, the one named last changes fastest.
Arguments:
- queries: bfloat16 [48, 8192], P(('groups', 'attn'), 'ffn'), parts along dimension 0, may hold values from -450 to 450
- root_keys: bfloat16 [16384, 512], P(('groups', 'attn'), 'ffn'), parts along dimension 0, may hold values from -1 to 1
- root_values: bfloat16 [16384, 512], P(('groups', 'attn'), 'ffn'), parts along dimension 0, may hold values from -6 to 6
- suffix_keys: bfloat16 [96, 128, 512], P(('groups', 'attn'), None, 'ffn'), parts along dimension 0, may hold values from -15 to 15
- suffix_values: bfloat16 [96, 128, 512], P(('groups', 'attn'), None, 'ffn'), parts along dimension 0, may hold values from -6 to 6
- suffix_lengths: int32 [48], P('groups'), parts along dimension 0, may hold values from 1 to 256, as said below
- block_table: int32 [96], P('groups'), parts along dimension 0, may hold values from 0 to 47, each once
- norm_gain: bfloat16 [8192], P('ffn'), may hold values from 0.099609375 to 1.8984375
- w_gate_up: bfloat16 [8192, 2, 26624], P('ffn', None, 'attn'), may hold values from -0.0625 to 0.0625
- w_down: bfloat16 [26624, 8192], P('attn', 'ffn'), may hold values from -0.0390625 to 0.0390625
Outputs:
- mixed: bfloat16 [48, 8192], P(('groups', 'attn'), 'ffn'), parts along dimension 0
The draws below stay inside these ranges and needn't reach their ends.
There are 2 independent parts, one for each index of `groups`. The reference program is written for one: setup_inputs(seed, part) draws one part's arguments, and reference() takes and returns one part's arrays. A program takes and returns all parts, laid end to end along the dimension named above; an argument that names none is the same for every part. Nothing has to cross between parts.
Inputs may be any that keep to these rules, and one draw needn't show every extreme that they name: `suffix_lengths`: every request has at least one suffix position and some request has 256. `block_table`: each pool page is named once.
All inputs are finite; a program needn't handle non-finite values.
Results may differ from the reference program's by a relative error of at most 0.02.
Values may be sent and summed in bfloat16 or wider, within the bound.
A program may use at most 320 MiB of HBM per device.

```python
import jax
import jax.numpy as jnp
from jax import lax

HEAD_DIM = 128
HEADS = 64
KV_HEADS = 4
D = 8192
FF = 26624
REQUESTS = 24
ROOT = 8192
PAGE = 128
MAXBLK = 2
PAGES = 48


def shared_root(key):
    base = jax.random.normal(key, (ROOT, KV_HEADS * HEAD_DIM), jnp.float32)
    return jnp.clip(base, -4.0, 4.0) * 0.25


def draw_root_keys(key, part):
    base = shared_root(key)
    return base.astype(jnp.bfloat16)


def draw_queries(key, part):
    key = jax.random.fold_in(key, 13)
    drawn = jnp.clip(jax.random.normal(key, (REQUESTS, HEADS * HEAD_DIM), jnp.float32), -5.0, 5.0)
    return drawn.astype(jnp.bfloat16)


def draw_suffix_lengths(key, part):
    key = jax.random.fold_in(key, 17)
    lengths = jax.random.randint(key, (REQUESTS,), 1, MAXBLK * PAGE + 1)
    chosen = jax.random.randint(jax.random.fold_in(key, 1), (), 0, REQUESTS)
    return lengths.at[chosen].set(MAXBLK * PAGE)


def levels(rng, shape, pieces, low, largest):
    gain, own = 1.0, jax.random.fold_in(rng, 6)
    for position, parts in pieces:
        draws = jnp.exp(jax.random.uniform(jax.random.fold_in(own, position), (parts,), jnp.float32, low / len(pieces), largest / len(pieces)))
        gain = gain * jnp.repeat(draws, shape[position] // parts).reshape([-1 if axis == position else 1 for axis in range(len(shape))])
    return gain


def scatter_about(key, extent, deviation, bound, shards=(), held_as=jnp.bfloat16):
    level = levels(key, extent, shards, -0.22, 0.18) if shards else 1.0
    array = jax.random.normal(key, extent, jnp.float32) * deviation * level
    return jnp.minimum(jnp.maximum(array, -bound), bound).astype(held_as)


def setup_inputs(seed: int = 0, part: int = 0) -> dict:
    seeds = jax.random.split(jax.random.key(seed), 11)
    part_keys = jax.random.split(jax.random.fold_in(seeds[10], part), 11)
    queries = draw_queries(jax.random.fold_in(jax.random.fold_in(seeds[10], part), 71), part)
    root_keys = draw_root_keys(jax.random.fold_in(jax.random.fold_in(seeds[10], part), 71), part)
    root_values = scatter_about(part_keys[2], (ROOT, KV_HEADS * HEAD_DIM), 1.0, 6.0, ((0, 8), (1, 2)))
    suffix_keys = scatter_about(part_keys[3], (PAGES, PAGE, KV_HEADS * HEAD_DIM), 2.5, 15.0, ((0, 8), (2, 2)))
    suffix_values = scatter_about(part_keys[4], (PAGES, PAGE, KV_HEADS * HEAD_DIM), 1.0, 6.0, ((0, 8), (2, 2)))
    suffix_lengths = draw_suffix_lengths(jax.random.fold_in(jax.random.fold_in(seeds[10], part), 71), part)
    block_table = jax.random.permutation(part_keys[6], PAGES).astype(jnp.int32)
    norm_gain = jnp.clip(1.0 + 0.18 * jax.random.normal(seeds[7], (D,), jnp.float32), 0.099609375, 1.8984375).astype(jnp.bfloat16)
    w_gate_up = scatter_about(seeds[8], (D, 2, FF), D ** -0.5, 0.0625, ((0, 2), (2, 8)))
    w_down = scatter_about(seeds[9], (FF, D), FF ** -0.5, 0.0390625, ((0, 8), (1, 2)))
    return dict(queries=queries, root_keys=root_keys, root_values=root_values, suffix_keys=suffix_keys, suffix_values=suffix_values, suffix_lengths=suffix_lengths, block_table=block_table, norm_gain=norm_gain, w_gate_up=w_gate_up, w_down=w_down)


def reference(queries, root_keys, root_values, suffix_keys, suffix_values, suffix_lengths, block_table, norm_gain, w_gate_up, w_down):
    group = HEADS // KV_HEADS
    scale = HEAD_DIM ** (-0.5)
    span = MAXBLK * PAGE
    table = block_table.reshape(REQUESTS, MAXBLK)
    tail_keys = suffix_keys[table].reshape(REQUESTS, span, KV_HEADS, HEAD_DIM)
    tail_values = suffix_values[table].reshape(REQUESTS, span, KV_HEADS, HEAD_DIM)
    live = jnp.arange(span, dtype=jnp.int32)[None, :] < suffix_lengths[:, None]
    keys = root_keys.astype(jnp.float32).reshape(ROOT, KV_HEADS, HEAD_DIM)
    values = root_values.astype(jnp.float32).reshape(ROOT, KV_HEADS, HEAD_DIM)

    def attend(item):
        query, own_keys, own_values, own_live = item
        query_f = query.astype(jnp.float32).reshape(KV_HEADS, group, HEAD_DIM)
        root_scores = jnp.einsum('kgd,tkd->kgt', query_f, keys) * scale
        tail_scores = jnp.einsum('kgd,tkd->kgt', query_f, own_keys.astype(jnp.float32)) * scale
        tail_scores = jnp.where(own_live[None, None, :], tail_scores, -1e+30)
        top = jnp.maximum(root_scores.max(-1), tail_scores.max(-1))
        root_weights = jnp.exp(root_scores - top[..., None])
        tail_weights = jnp.where(own_live[None, None, :], jnp.exp(tail_scores - top[..., None]), 0.0)
        total = root_weights.sum(-1) + tail_weights.sum(-1)
        summed = jnp.einsum('kgt,tkd->kgd', root_weights.astype(jnp.bfloat16).astype(jnp.float32), values)
        summed = summed + jnp.einsum('kgt,tkd->kgd', tail_weights.astype(jnp.bfloat16).astype(jnp.float32), own_values.astype(jnp.float32))
        return (summed / total[..., None]).reshape(HEADS * HEAD_DIM)
    attended = lax.map(attend, (queries, tail_keys, tail_values, live))
    mean_square = lax.optimization_barrier(jnp.mean(attended * attended, axis=1, keepdims=True))
    hidden = (attended * lax.rsqrt(mean_square + 1e-05) * norm_gain.astype(jnp.float32)[None, :]).astype(jnp.bfloat16)
    gate_up = jnp.dot(hidden, w_gate_up.reshape(D, 2 * FF), preferred_element_type=jnp.float32)
    activation = (jax.nn.silu(gate_up[:, :FF]) * gate_up[:, FF:]).astype(jnp.bfloat16)
    return jnp.dot(activation, w_down, preferred_element_type=jnp.float32).astype(jnp.bfloat16)
```

```python
import functools

import jax
import jax.numpy as jnp
from jax import lax
from jax.experimental import pallas as pl
from jax.experimental.pallas import tpu as pltpu
from jax.sharding import PartitionSpec as P

HEAD_DIM = 128
PAGE = 128
MAXBLK = 2
MESH = pl.DeviceIdType.MESH


def enter(axes):
    barrier = pltpu.get_barrier_semaphore()
    greeted = 0
    for axis, size in axes:
        me = lax.axis_index(axis)
        for d in range(1, size):
            pl.semaphore_signal(
                barrier, inc=1, device_id={axis: lax.rem(me + d, size)}, device_id_type=MESH
            )
            greeted += 1
    pl.semaphore_wait(barrier, greeted)


def exchange(axis, size, source, target, sems):
    me = lax.axis_index(axis)
    copies = []
    for d in range(1, size):
        peer = lax.rem(me + d, size)
        copy = pltpu.make_async_remote_copy(
            src_ref=source(peer),
            dst_ref=target,
            send_sem=sems.at[0, d],
            recv_sem=sems.at[1, d],
            device_id={axis: peer},
            device_id_type=MESH,
        )
        copy.start()
        copies.append(copy)
    return copies


def attention_kernel(
    n, f, kv, group, q_ref, rk_ref, rv_ref, sk_ref, sv_ref, bias_ref, gain_ref, out_ref,
    qbuf, psend, precv, ssend, srecv, sqsend, sqrecv, hbuf,
    q_sems, p_sems, s_sems, sq_sems, h_sems,
):
    me = lax.axis_index("attn")
    mf = lax.axis_index("ffn")
    rows = q_ref.shape[1]
    req = rows // group
    scale = HEAD_DIM ** (-0.5)
    features = kv * group * HEAD_DIM * f
    if srecv.shape[0] > n:
        srecv[n:] = jnp.zeros_like(srecv[n:])
    enter((("attn", n), ("ffn", f)))
    sent = exchange("attn", n, lambda peer: q_ref, qbuf.at[me], q_sems)
    qbuf[me] = q_ref[...]
    for copy in sent:
        copy.wait()

    at_once = 4 if n % 4 == 0 else 1
    paged = sk_ref.shape[0]

    def block(b, carry):
        stats = []
        for k in range(kv):
            cols = slice(k * HEAD_DIM, (k + 1) * HEAD_DIM)
            query = qbuf[pl.ds(b * at_once, at_once), k].reshape(at_once * rows, HEAD_DIM)
            across = (((1,), (1,)), ((), ()))
            root = scale * lax.dot_general(
                query, rk_ref[:, cols], across, preferred_element_type=jnp.float32
            )
            page = scale * lax.dot_general(
                query, sk_ref[:, cols], across, preferred_element_type=jnp.float32
            )
            page = page.reshape(at_once * req, group, paged)
            page = page + bias_ref[pl.ds(b * at_once * req, at_once * req)]
            page = page.reshape(at_once * rows, paged)
            peak = jnp.maximum(
                jnp.max(root, axis=1, keepdims=True), jnp.max(page, axis=1, keepdims=True)
            )
            root = jnp.exp(root - peak)
            page = jnp.exp(page - peak)
            total = jnp.sum(root, axis=1, keepdims=True) + jnp.sum(page, axis=1, keepdims=True)
            summed = jnp.dot(
                root.astype(jnp.bfloat16), rv_ref[:, cols], preferred_element_type=jnp.float32
            ) + jnp.dot(
                page.astype(jnp.bfloat16), sv_ref[:, cols], preferred_element_type=jnp.float32
            )
            mean = (summed / total).astype(jnp.bfloat16)
            psend[pl.ds(b * at_once, at_once), k] = mean.reshape(at_once, rows, HEAD_DIM)
            stats.append(peak + jnp.log(total))
        lane = lax.broadcasted_iota(jnp.int32, (rows, 128), 1)
        for i in range(at_once):
            part = slice(i * rows, (i + 1) * rows)
            wide = jnp.broadcast_to(stats[0][part], (rows, 128))
            for k in range(1, kv):
                wide = jnp.where(lane % 8 >= k * (8 // kv), stats[k][part], wide)
            wide = jnp.concatenate([wide, jnp.zeros((128 - rows, 128), jnp.float32)], axis=0)
            ssend[b * at_once + i] = wide.T[:8]
        return carry

    lax.fori_loop(0, n // at_once, block, 0)

    sent = exchange("attn", n, lambda peer: ssend.at[peer], srecv.at[me], s_sems)
    sent += exchange("attn", n, lambda peer: psend.at[peer], precv.at[me], p_sems)
    srecv[me] = ssend[me]
    precv[me] = psend[me]
    for copy in sent:
        copy.wait()
    turned = [
        srecv[c * 16 : (c + 1) * 16].reshape(128, 128).T[:rows] for c in range(srecv.shape[0] // 16)
    ]
    attended = []
    for k in range(kv):
        def level(j):
            at = (j % 16) * 8 + k * (8 // kv)
            return turned[j // 16][:, at : at + 1]

        top = level(0)
        for j in range(1, n):
            top = jnp.maximum(top, level(j))
        total = jnp.zeros((rows, 1), jnp.float32)
        summed = jnp.zeros((rows, HEAD_DIM), jnp.float32)
        for j in range(n):
            weight = jnp.exp(level(j) - top)
            total = total + weight
            summed = summed + weight * precv[j, k].astype(jnp.float32)
        attended.append((summed / total).reshape(req, group, HEAD_DIM))
    squares = jnp.zeros((req, 1, 1), jnp.float32)
    for k in range(kv):
        lanes = jnp.sum(attended[k] * attended[k], axis=2, keepdims=True)
        squares = squares + jnp.sum(lanes, axis=1, keepdims=True)
    sqsend[...] = jnp.broadcast_to(squares, sqsend.shape)
    sent = exchange("ffn", f, lambda peer: sqsend, sqrecv.at[mf], sq_sems)
    sqrecv[mf] = sqsend[...]
    for copy in sent:
        copy.wait()
    whole = sqrecv[0]
    for j in range(1, f):
        whole = whole + sqrecv[j]
    factor = lax.rsqrt(whole / features + 1e-05)[:, :1, :]
    for k in range(kv):
        hidden = attended[k] * factor * gain_ref[k].astype(jnp.float32)[None]
        hbuf[me, k] = hidden.reshape(rows, HEAD_DIM).astype(jnp.bfloat16)
    sent = exchange("attn", n, lambda peer: hbuf.at[me], hbuf.at[me], h_sems)
    for copy in sent:
        copy.wait()
    out_ref[...] = hbuf[...]


def ffn_kernel(
    n, f, pieces, lhs_ref, w_ref, down_ref, out_ref,
    acc, held, xsend, xrecv, active, result, osend, orecv, d_sems, x_sems, o_sems,
):
    step = pl.program_id(0)
    me = lax.axis_index("attn")
    mf = lax.axis_index("ffn")
    chunk, _, units = w_ref.shape
    count = acc.shape[0] // 2
    req = count // n
    piece = held.shape[0] // pieces

    def fetch(i):
        at = pl.ds(pl.multiple_of(i * piece, piece), piece)
        return pltpu.make_async_copy(down_ref.at[at], held.at[at], d_sems.at[i])

    @pl.when(step == 0)
    def _():
        enter((("attn", n), ("ffn", f)))
        acc[...] = jnp.zeros_like(acc)

    @pl.when(step < pieces)
    def _():
        fetch(step).start()

    acc[...] += jnp.dot(
        lhs_ref[...], w_ref[...].reshape(2 * chunk, units), preferred_element_type=jnp.float32
    )

    @pl.when(step == pl.num_programs(0) - 1)
    def _():
        xsend[...] = acc[...].astype(jnp.bfloat16)
        sent = exchange("ffn", f, lambda peer: xsend, xrecv.at[mf], x_sems)
        for copy in sent:
            copy.wait()
        total = acc[...]
        for d in range(1, f):
            total = total + xrecv[lax.rem(mf + d, f)].astype(jnp.float32)
        gate = total[:count]
        active[...] = (gate * jax.nn.sigmoid(gate) * total[count:]).astype(jnp.bfloat16)

        def landed(i, carry):
            fetch(i).wait()
            return carry

        lax.fori_loop(0, pieces, landed, 0)
        width = result.shape[1]
        tile = 512 if width % 512 == 0 else width

        def columns(c, carry):
            at = pl.ds(pl.multiple_of(c * tile, tile), tile)
            result[:, at] = jnp.dot(
                active[...], held[:, at], preferred_element_type=jnp.float32
            )
            return carry

        lax.fori_loop(0, width // tile, columns, 0)
        for j in range(n):
            osend[j] = result[j * req : (j + 1) * req].astype(jnp.bfloat16)
        sent = exchange("attn", n, lambda peer: osend.at[peer], orecv.at[me], o_sems)
        orecv[me] = osend[me]
        for copy in sent:
            copy.wait()
        mixed = orecv[0].astype(jnp.float32)
        for j in range(1, n):
            mixed = mixed + orecv[j].astype(jnp.float32)
        out_ref[...] = mixed.astype(jnp.bfloat16)


def per_device(
    n, f, queries, root_keys, root_values, suffix_keys, suffix_values, suffix_lengths,
    block_table, norm_gain, w_gate_up, w_down,
):
    req = queries.shape[0]
    kv = root_keys.shape[1] // HEAD_DIM
    heads = queries.shape[1] // HEAD_DIM
    group = heads // kv
    rows = req * group
    count = req * n
    pages = suffix_keys.shape[0]
    width = heads * HEAD_DIM

    mine = lax.axis_index("attn") * pages + jnp.arange(pages, dtype=jnp.int32)
    offset = jnp.arange(MAXBLK, dtype=jnp.int32) * PAGE
    room = jnp.clip(suffix_lengths[:, None] - offset[None, :], 0, PAGE)
    matches = block_table.reshape(count, MAXBLK)[:, :, None] == mine[None, None, :]
    valid = jnp.sum(jnp.where(matches, room[:, :, None], 0), axis=1)
    alive = jnp.arange(PAGE, dtype=jnp.int32)[None, None, :] < valid[:, :, None]
    bias = jnp.where(alive, 0.0, -1e30).astype(jnp.float32).reshape(count, 1, pages * PAGE)

    blocked = queries.reshape(req, kv, group, HEAD_DIM).transpose(1, 0, 2, 3)
    blocked = blocked.reshape(kv, rows, HEAD_DIM)
    vmem = pl.BlockSpec(memory_space=pltpu.VMEM)
    share = (n, kv, rows, HEAD_DIM)

    def pair(size):
        return pltpu.SemaphoreType.DMA((2, size))

    hidden = pl.pallas_call(
        functools.partial(attention_kernel, n, f, kv, group),
        out_shape=jax.ShapeDtypeStruct(share, jnp.bfloat16),
        in_specs=[vmem] * 7,
        out_specs=vmem,
        scratch_shapes=[
            pltpu.VMEM(share, jnp.bfloat16),
            pltpu.VMEM(share, jnp.bfloat16),
            pltpu.VMEM(share, jnp.bfloat16),
            pltpu.VMEM((n, 8, 128), jnp.float32),
            pltpu.VMEM(((n + 15) // 16 * 16, 8, 128), jnp.float32),
            pltpu.VMEM((req, 8, 128), jnp.float32),
            pltpu.VMEM((f, req, 8, 128), jnp.float32),
            pltpu.VMEM(share, jnp.bfloat16),
            pair(n),
            pair(n),
            pair(n),
            pair(f),
            pair(n),
        ],
        compiler_params=pltpu.CompilerParams(
            collective_id=0, has_side_effects=True, vmem_limit_bytes=40 << 20
        ),
    )(
        blocked,
        root_keys,
        root_values,
        suffix_keys.reshape(pages * PAGE, kv * HEAD_DIM),
        suffix_values.reshape(pages * PAGE, kv * HEAD_DIM),
        bias,
        norm_gain.reshape(kv, group, HEAD_DIM),
    )
    hidden = hidden.reshape(n, kv, req, group, HEAD_DIM).transpose(0, 2, 1, 3, 4)
    hidden = hidden.reshape(count, width)
    blank = jnp.zeros_like(hidden)
    lhs = jnp.concatenate(
        [
            jnp.stack([hidden, blank], axis=-1).reshape(count, 2 * width),
            jnp.stack([blank, hidden], axis=-1).reshape(count, 2 * width),
        ],
        axis=0,
    )

    units = w_gate_up.shape[2]
    chunk = 128
    steps = width // chunk
    pieces = 1
    for p in range(1, steps + 1):
        if units % (16 * p) == 0:
            pieces = p
    return pl.pallas_call(
        functools.partial(ffn_kernel, n, f, pieces),
        grid=(steps,),
        out_shape=jax.ShapeDtypeStruct((req, width), jnp.bfloat16),
        in_specs=[
            pl.BlockSpec((2 * count, 2 * chunk), lambda i: (0, i)),
            pl.BlockSpec((chunk, 2, units), lambda i: (i, 0, 0)),
            pl.BlockSpec(memory_space=pl.ANY),
        ],
        out_specs=pl.BlockSpec((req, width), lambda i: (0, 0)),
        scratch_shapes=[
            pltpu.VMEM((2 * count, units), jnp.float32),
            pltpu.VMEM((units, width), jnp.bfloat16),
            pltpu.VMEM((2 * count, units), jnp.bfloat16),
            pltpu.VMEM((f, 2 * count, units), jnp.bfloat16),
            pltpu.VMEM((count, units), jnp.bfloat16),
            pltpu.VMEM((count, width), jnp.float32),
            pltpu.VMEM((n, req, width), jnp.bfloat16),
            pltpu.VMEM((n, req, width), jnp.bfloat16),
            pltpu.SemaphoreType.DMA((pieces,)),
            pair(f),
            pair(n),
        ],
        compiler_params=pltpu.CompilerParams(
            collective_id=1, has_side_effects=True, vmem_limit_bytes=52 << 20
        ),
    )(lhs, w_gate_up, w_down)


def solution(mesh):
    return jax.shard_map(
        functools.partial(per_device, mesh.shape["attn"], mesh.shape["ffn"]),
        mesh=mesh,
        in_specs=(
            P(("groups", "attn"), "ffn"),
            P(("groups", "attn"), "ffn"),
            P(("groups", "attn"), "ffn"),
            P(("groups", "attn"), None, "ffn"),
            P(("groups", "attn"), None, "ffn"),
            P("groups"),
            P("groups"),
            P("ffn"),
            P("ffn", None, "attn"),
            P("attn", "ffn"),
        ),
        out_specs=P(("groups", "attn"), "ffn"),
        check_vma=False,
    )
```

```python
import functools

import jax
import jax.numpy as jnp
from jax import lax
from jax.experimental import pallas as pl
from jax.experimental.pallas import tpu as pltpu
from jax.sharding import PartitionSpec as P

HEAD_DIM = 128
PAGE = 128
MAXBLK = 2
MESH = pl.DeviceIdType.MESH


def enter(axes):
    barrier = pltpu.get_barrier_semaphore()
    greeted = 0
    for axis, size in axes:
        me = lax.axis_index(axis)
        for d in range(1, size):
            pl.semaphore_signal(
                barrier, inc=1, device_id={axis: lax.rem(me + d, size)}, device_id_type=MESH
            )
            greeted += 1
    pl.semaphore_wait(barrier, greeted)


def exchange(axis, size, source, target, sems):
    me = lax.axis_index(axis)
    copies = []
    for d in range(1, size):
        peer = lax.rem(me + d, size)
        copy = pltpu.make_async_remote_copy(
            src_ref=source(peer),
            dst_ref=target,
            send_sem=sems.at[0, d],
            recv_sem=sems.at[1, d],
            device_id={axis: peer},
            device_id_type=MESH,
        )
        copy.start()
        copies.append(copy)
    return copies


def attention_kernel(
    n, f, kv, group, q_ref, rk_ref, rv_ref, sk_ref, sv_ref, bias_ref, gain_ref, out_ref,
    qbuf, psend, precv, ssend, srecv, sqsend, sqrecv, hbuf,
    q_sems, p_sems, s_sems, sq_sems, h_sems,
):
    me = lax.axis_index("attn")
    mf = lax.axis_index("ffn")
    rows = q_ref.shape[1]
    req = rows // group
    scale = HEAD_DIM ** (-0.5)
    features = kv * group * HEAD_DIM * f
    if srecv.shape[0] > n:
        srecv[n:] = jnp.zeros_like(srecv[n:])
    enter((("attn", n), ("ffn", f)))
    sent = exchange("attn", n, lambda peer: q_ref, qbuf.at[me], q_sems)
    qbuf[me] = q_ref[...]
    for copy in sent:
        copy.wait()

    at_once = 4 if n % 4 == 0 else 1
    paged = sk_ref.shape[0]

    def block(b, carry):
        stats = []
        for k in range(kv):
            cols = slice(k * HEAD_DIM, (k + 1) * HEAD_DIM)
            query = qbuf[pl.ds(b * at_once, at_once), k].reshape(at_once * rows, HEAD_DIM)
            across = (((1,), (1,)), ((), ()))
            root = scale * lax.dot_general(
                query, rk_ref[:, cols], across, preferred_element_type=jnp.float32
            )
            page = scale * lax.dot_general(
                query, sk_ref[:, cols], across, preferred_element_type=jnp.float32
            )
            page = page.reshape(at_once * req, group, paged)
            page = page + bias_ref[pl.ds(b * at_once * req, at_once * req)]
            page = page.reshape(at_once * rows, paged)
            peak = jnp.maximum(
                jnp.max(root, axis=1, keepdims=True), jnp.max(page, axis=1, keepdims=True)
            )
            root = jnp.exp(root - peak)
            page = jnp.exp(page - peak)
            total = jnp.sum(root, axis=1, keepdims=True) + jnp.sum(page, axis=1, keepdims=True)
            summed = jnp.dot(
                root.astype(jnp.bfloat16), rv_ref[:, cols], preferred_element_type=jnp.float32
            ) + jnp.dot(
                page.astype(jnp.bfloat16), sv_ref[:, cols], preferred_element_type=jnp.float32
            )
            mean = (summed / total).astype(jnp.bfloat16)
            psend[pl.ds(b * at_once, at_once), k] = mean.reshape(at_once, rows, HEAD_DIM)
            stats.append(peak + jnp.log(total))
        lane = lax.broadcasted_iota(jnp.int32, (rows, 128), 1)
        for i in range(at_once):
            part = slice(i * rows, (i + 1) * rows)
            wide = jnp.broadcast_to(stats[0][part], (rows, 128))
            for k in range(1, kv):
                wide = jnp.where(lane % 8 >= k * (8 // kv), stats[k][part], wide)
            wide = jnp.concatenate([wide, jnp.zeros((128 - rows, 128), jnp.float32)], axis=0)
            ssend[b * at_once + i] = wide.T[:8]
        return carry

    lax.fori_loop(0, n // at_once, block, 0)

    sent = exchange("attn", n, lambda peer: ssend.at[peer], srecv.at[me], s_sems)
    sent += exchange("attn", n, lambda peer: psend.at[peer], precv.at[me], p_sems)
    srecv[me] = ssend[me]
    precv[me] = psend[me]
    for copy in sent:
        copy.wait()
    turned = [
        srecv[c * 16 : (c + 1) * 16].reshape(128, 128).T[:rows] for c in range(srecv.shape[0] // 16)
    ]
    attended = []
    for k in range(kv):
        def level(j):
            at = (j % 16) * 8 + k * (8 // kv)
            return turned[j // 16][:, at : at + 1]

        top = level(0)
        for j in range(1, n):
            top = jnp.maximum(top, level(j))
        total = jnp.zeros((rows, 1), jnp.float32)
        summed = jnp.zeros((rows, HEAD_DIM), jnp.float32)
        for j in range(n):
            weight = jnp.exp(level(j) - top)
            total = total + weight
            summed = summed + weight * precv[j, k].astype(jnp.float32)
        attended.append((summed / total).reshape(req, group, HEAD_DIM))
    squares = jnp.zeros((req, 1, 1), jnp.float32)
    for k in range(kv):
        lanes = jnp.sum(attended[k] * attended[k], axis=2, keepdims=True)
        squares = squares + jnp.sum(lanes, axis=1, keepdims=True)
    sqsend[...] = jnp.broadcast_to(squares, sqsend.shape)
    sent = exchange("ffn", f, lambda peer: sqsend, sqrecv.at[mf], sq_sems)
    sqrecv[mf] = sqsend[...]
    for copy in sent:
        copy.wait()
    whole = sqrecv[0]
    for j in range(1, f):
        whole = whole + sqrecv[j]
    factor = lax.rsqrt(whole / features + 1e-05)[:, :1, :]
    for k in range(kv):
        hidden = attended[k] * factor * gain_ref[k].astype(jnp.float32)[None]
        hbuf[me, k] = hidden.reshape(rows, HEAD_DIM).astype(jnp.bfloat16)
    sent = exchange("attn", n, lambda peer: hbuf.at[me], hbuf.at[me], h_sems)
    for copy in sent:
        copy.wait()
    if out_ref is not None:
        out_ref[...] = hbuf[...]


def fused_kernel(
    n, f, kv, group, q_ref, rk_ref, rv_ref, sk_ref, sv_ref, bias_ref, gain_ref,
    w_ref, down_ref, out_ref,
    qbuf, psend, precv, ssend, srecv, sqsend, sqrecv, hbuf,
    q_sems, p_sems, s_sems, sq_sems, h_sems,
    ring, w_sems, lhs, acc, xsend, xrecv, active, result, osend, orecv, x_sems, o_sems,
):
    me = lax.axis_index("attn")
    mf = lax.axis_index("ffn")
    width, _, units = w_ref.shape
    slots = ring.shape[0]
    tiles = units // 128
    steps = width // 256
    late = steps - slots
    count = acc.shape[0] // 2
    req = count // n
    pairs = w_ref.reshape(2 * width, units)

    def up_load(i):
        slot = lax.rem(i, slots)
        at = pl.ds(pl.multiple_of(i * 512, 512), 512)
        return [
            pltpu.make_async_copy(
                pairs.at[at, pl.ds(c * 128, 128)],
                ring.at[slot, pl.ds(c * 512, 512)],
                w_sems.at[slot, c],
            )
            for c in range(tiles)
        ]

    def down_load(d):
        return [
            pltpu.make_async_copy(
                down_ref.at[:, pl.ds(pl.multiple_of((4 * d + t) * 128, 128), 128)],
                ring.at[late + d, pl.ds(t * units, units)],
                w_sems.at[late + d, t],
            )
            for t in range(4)
        ]

    def first(i, carry):
        for copy in up_load(i):
            copy.start()
        return carry

    lax.fori_loop(0, slots, first, 0)
    attention_kernel(
        n, f, kv, group, q_ref, rk_ref, rv_ref, sk_ref, sv_ref, bias_ref, gain_ref, None,
        qbuf, psend, precv, ssend, srecv, sqsend, sqrecv, hbuf,
        q_sems, p_sems, s_sems, sq_sems, h_sems,
    )

    rows = count * group
    row = lax.broadcasted_iota(jnp.int32, (rows, rows), 0)
    column = lax.broadcasted_iota(jnp.int32, (rows, rows), 1)
    order = jnp.where(column == (row % count) * group + row // count, 1.0, 0.0)
    order = order.astype(jnp.bfloat16)
    feature = lax.broadcasted_iota(jnp.int32, (128, 256), 0)
    spread = lax.broadcasted_iota(jnp.int32, (128, 256), 1)
    for k in range(kv):
        held = hbuf[:, k].reshape(rows, HEAD_DIM)
        held = jnp.dot(order, held, preferred_element_type=jnp.float32).astype(jnp.bfloat16)
        halves = []
        for g in range(2):
            place = jnp.where(spread == 2 * feature + g, 1.0, 0.0).astype(jnp.bfloat16)
            half = jnp.dot(held, place, preferred_element_type=jnp.float32)
            halves.append(half.reshape(group, count, 256))
        both = jnp.concatenate(halves, axis=1).astype(jnp.bfloat16)
        lhs[k * group : (k + 1) * group] = both
    acc[...] = jnp.zeros_like(acc)

    def multiply(i):
        slot = lax.rem(i, slots)
        for copy in up_load(i):
            copy.wait()
        left = jnp.concatenate([lhs[2 * i], lhs[2 * i + 1]], axis=1)
        for c in range(0, tiles, 2):
            right = jnp.concatenate(
                [ring[slot, c * 512 : (c + 1) * 512], ring[slot, (c + 1) * 512 : (c + 2) * 512]],
                axis=1,
            )
            acc[:, c * 128 : (c + 2) * 128] += jnp.dot(
                left, right, preferred_element_type=jnp.float32
            )

    def early(i, carry):
        multiply(i)
        for copy in up_load(i + slots):
            copy.start()
        return carry

    def middle(i, carry):
        multiply(i)
        for copy in down_load(i - late):
            copy.start()
        return carry

    def final(i, carry):
        multiply(i)
        return carry

    lax.fori_loop(0, late, early, 0)
    lax.fori_loop(late, slots, middle, 0)
    lax.fori_loop(slots, steps, final, 0)

    xsend[...] = acc[...].astype(jnp.bfloat16)
    for copy in exchange("ffn", f, lambda peer: xsend, xrecv.at[mf], x_sems):
        copy.wait()
    total = acc[...]
    for d in range(1, f):
        total = total + xrecv[lax.rem(mf + d, f)].astype(jnp.float32)
    gate = total[:count]
    active[...] = (gate * jax.nn.sigmoid(gate) * total[count:]).astype(jnp.bfloat16)

    def columns(d, carry):
        for copy in down_load(d):
            copy.wait()
        for t in range(0, 4, 2):
            right = jnp.concatenate(
                [
                    ring[late + d, t * units : (t + 1) * units],
                    ring[late + d, (t + 1) * units : (t + 2) * units],
                ],
                axis=1,
            )
            at = pl.ds(pl.multiple_of(d * 512 + t * 128, 256), 256)
            result[:, at] = jnp.dot(active[...], right, preferred_element_type=jnp.float32)
        return carry

    lax.fori_loop(0, width // 512, columns, 0)
    for j in range(n):
        osend[j] = result[j * req : (j + 1) * req].astype(jnp.bfloat16)
    sent = exchange("attn", n, lambda peer: osend.at[peer], orecv.at[me], o_sems)
    orecv[me] = osend[me]
    for copy in sent:
        copy.wait()
    mixed = orecv[0].astype(jnp.float32)
    for j in range(1, n):
        mixed = mixed + orecv[j].astype(jnp.float32)
    out_ref[...] = mixed.astype(jnp.bfloat16)


def ffn_kernel(
    n, f, pieces, lhs_ref, w_ref, down_ref, out_ref,
    acc, held, xsend, xrecv, active, result, osend, orecv, d_sems, x_sems, o_sems,
):
    step = pl.program_id(0)
    me = lax.axis_index("attn")
    mf = lax.axis_index("ffn")
    chunk, _, units = w_ref.shape
    count = acc.shape[0] // 2
    req = count // n
    piece = held.shape[0] // pieces

    def fetch(i):
        at = pl.ds(pl.multiple_of(i * piece, piece), piece)
        return pltpu.make_async_copy(down_ref.at[at], held.at[at], d_sems.at[i])

    @pl.when(step == 0)
    def _():
        enter((("attn", n), ("ffn", f)))
        acc[...] = jnp.zeros_like(acc)

    @pl.when(step < pieces)
    def _():
        fetch(step).start()

    acc[...] += jnp.dot(
        lhs_ref[...], w_ref[...].reshape(2 * chunk, units), preferred_element_type=jnp.float32
    )

    @pl.when(step == pl.num_programs(0) - 1)
    def _():
        xsend[...] = acc[...].astype(jnp.bfloat16)
        sent = exchange("ffn", f, lambda peer: xsend, xrecv.at[mf], x_sems)
        for copy in sent:
            copy.wait()
        total = acc[...]
        for d in range(1, f):
            total = total + xrecv[lax.rem(mf + d, f)].astype(jnp.float32)
        gate = total[:count]
        active[...] = (gate * jax.nn.sigmoid(gate) * total[count:]).astype(jnp.bfloat16)

        def landed(i, carry):
            fetch(i).wait()
            return carry

        lax.fori_loop(0, pieces, landed, 0)
        width = result.shape[1]
        tile = 512 if width % 512 == 0 else width

        def columns(c, carry):
            at = pl.ds(pl.multiple_of(c * tile, tile), tile)
            result[:, at] = jnp.dot(
                active[...], held[:, at], preferred_element_type=jnp.float32
            )
            return carry

        lax.fori_loop(0, width // tile, columns, 0)
        for j in range(n):
            osend[j] = result[j * req : (j + 1) * req].astype(jnp.bfloat16)
        sent = exchange("attn", n, lambda peer: osend.at[peer], orecv.at[me], o_sems)
        orecv[me] = osend[me]
        for copy in sent:
            copy.wait()
        mixed = orecv[0].astype(jnp.float32)
        for j in range(1, n):
            mixed = mixed + orecv[j].astype(jnp.float32)
        out_ref[...] = mixed.astype(jnp.bfloat16)


def per_device(
    n, f, queries, root_keys, root_values, suffix_keys, suffix_values, suffix_lengths,
    block_table, norm_gain, w_gate_up, w_down,
):
    req = queries.shape[0]
    kv = root_keys.shape[1] // HEAD_DIM
    heads = queries.shape[1] // HEAD_DIM
    group = heads // kv
    rows = req * group
    count = req * n
    pages = suffix_keys.shape[0]
    width = heads * HEAD_DIM

    mine = lax.axis_index("attn") * pages + jnp.arange(pages, dtype=jnp.int32)
    offset = jnp.arange(MAXBLK, dtype=jnp.int32) * PAGE
    room = jnp.clip(suffix_lengths[:, None] - offset[None, :], 0, PAGE)
    matches = block_table.reshape(count, MAXBLK)[:, :, None] == mine[None, None, :]
    valid = jnp.sum(jnp.where(matches, room[:, :, None], 0), axis=1)
    alive = jnp.arange(PAGE, dtype=jnp.int32)[None, None, :] < valid[:, :, None]
    bias = jnp.where(alive, 0.0, -1e30).astype(jnp.float32).reshape(count, 1, pages * PAGE)

    blocked = queries.reshape(req, kv, group, HEAD_DIM).transpose(1, 0, 2, 3)
    blocked = blocked.reshape(kv, rows, HEAD_DIM)
    vmem = pl.BlockSpec(memory_space=pltpu.VMEM)
    share = (n, kv, rows, HEAD_DIM)

    def pair(size):
        return pltpu.SemaphoreType.DMA((2, size))

    operands = (
        blocked,
        root_keys,
        root_values,
        suffix_keys.reshape(pages * PAGE, kv * HEAD_DIM),
        suffix_values.reshape(pages * PAGE, kv * HEAD_DIM),
        bias,
        norm_gain.reshape(kv, group, HEAD_DIM),
    )
    scratch = [
        pltpu.VMEM(share, jnp.bfloat16),
        pltpu.VMEM(share, jnp.bfloat16),
        pltpu.VMEM(share, jnp.bfloat16),
        pltpu.VMEM((n, 8, 128), jnp.float32),
        pltpu.VMEM(((n + 15) // 16 * 16, 8, 128), jnp.float32),
        pltpu.VMEM((req, 8, 128), jnp.float32),
        pltpu.VMEM((f, req, 8, 128), jnp.float32),
        pltpu.VMEM(share, jnp.bfloat16),
        pair(n),
        pair(n),
        pair(n),
        pair(f),
        pair(n),
    ]
    units = w_gate_up.shape[2]
    if units % 256 == 0 and width % 2048 == 0 and count % 8 == 0:
        slots = width // 256 * 3 // 4
        return pl.pallas_call(
            functools.partial(fused_kernel, n, f, kv, group),
            out_shape=jax.ShapeDtypeStruct((req, width), jnp.bfloat16),
            in_specs=[vmem] * 7 + [pl.BlockSpec(memory_space=pl.ANY)] * 2,
            out_specs=vmem,
            scratch_shapes=scratch
            + [
                pltpu.VMEM((slots, 4 * units, 128), jnp.bfloat16),
                pltpu.SemaphoreType.DMA((slots, units // 128)),
                pltpu.VMEM((heads, 2 * count, 256), jnp.bfloat16),
                pltpu.VMEM((2 * count, units), jnp.float32),
                pltpu.VMEM((2 * count, units), jnp.bfloat16),
                pltpu.VMEM((f, 2 * count, units), jnp.bfloat16),
                pltpu.VMEM((count, units), jnp.bfloat16),
                pltpu.VMEM((count, width), jnp.float32),
                pltpu.VMEM((n, req, width), jnp.bfloat16),
                pltpu.VMEM((n, req, width), jnp.bfloat16),
                pair(f),
                pair(n),
            ],
            compiler_params=pltpu.CompilerParams(
                collective_id=2, has_side_effects=True, vmem_limit_bytes=58 << 20
            ),
        )(*operands, w_gate_up, w_down)
    hidden = pl.pallas_call(
        functools.partial(attention_kernel, n, f, kv, group),
        out_shape=jax.ShapeDtypeStruct(share, jnp.bfloat16),
        in_specs=[vmem] * 7,
        out_specs=vmem,
        scratch_shapes=scratch,
        compiler_params=pltpu.CompilerParams(
            collective_id=0, has_side_effects=True, vmem_limit_bytes=40 << 20
        ),
    )(*operands)
    hidden = hidden.reshape(n, kv, req, group, HEAD_DIM).transpose(0, 2, 1, 3, 4)
    hidden = hidden.reshape(count, width)
    blank = jnp.zeros_like(hidden)
    lhs = jnp.concatenate(
        [
            jnp.stack([hidden, blank], axis=-1).reshape(count, 2 * width),
            jnp.stack([blank, hidden], axis=-1).reshape(count, 2 * width),
        ],
        axis=0,
    )

    chunk = 128
    steps = width // chunk
    pieces = 1
    for p in range(1, steps + 1):
        if units % (16 * p) == 0:
            pieces = p
    return pl.pallas_call(
        functools.partial(ffn_kernel, n, f, pieces),
        grid=(steps,),
        out_shape=jax.ShapeDtypeStruct((req, width), jnp.bfloat16),
        in_specs=[
            pl.BlockSpec((2 * count, 2 * chunk), lambda i: (0, i)),
            pl.BlockSpec((chunk, 2, units), lambda i: (i, 0, 0)),
            pl.BlockSpec(memory_space=pl.ANY),
        ],
        out_specs=pl.BlockSpec((req, width), lambda i: (0, 0)),
        scratch_shapes=[
            pltpu.VMEM((2 * count, units), jnp.float32),
            pltpu.VMEM((units, width), jnp.bfloat16),
            pltpu.VMEM((2 * count, units), jnp.bfloat16),
            pltpu.VMEM((f, 2 * count, units), jnp.bfloat16),
            pltpu.VMEM((count, units), jnp.bfloat16),
            pltpu.VMEM((count, width), jnp.float32),
            pltpu.VMEM((n, req, width), jnp.bfloat16),
            pltpu.VMEM((n, req, width), jnp.bfloat16),
            pltpu.SemaphoreType.DMA((pieces,)),
            pair(f),
            pair(n),
        ],
        compiler_params=pltpu.CompilerParams(
            collective_id=1, has_side_effects=True, vmem_limit_bytes=52 << 20
        ),
    )(lhs, w_gate_up, w_down)


def solution(mesh):
    return jax.shard_map(
        functools.partial(per_device, mesh.shape["attn"], mesh.shape["ffn"]),
        mesh=mesh,
        in_specs=(
            P(("groups", "attn"), "ffn"),
            P(("groups", "attn"), "ffn"),
            P(("groups", "attn"), "ffn"),
            P(("groups", "attn"), None, "ffn"),
            P(("groups", "attn"), None, "ffn"),
            P("groups"),
            P("groups"),
            P("ffn"),
            P("ffn", None, "attn"),
            P("attn", "ffn"),
        ),
        out_specs=P(("groups", "attn"), "ffn"),
        check_vma=False,
    )
```

```python
import functools

import jax
import jax.numpy as jnp
from jax import lax
from jax.experimental import pallas as pl
from jax.experimental.pallas import tpu as pltpu
from jax.sharding import PartitionSpec as P

HEAD_DIM = 128
PAGE = 128
MAXBLK = 2
MESH = pl.DeviceIdType.MESH


def enter(axes):
    barrier = pltpu.get_barrier_semaphore()
    greeted = 0
    for axis, size in axes:
        me = lax.axis_index(axis)
        for d in range(1, size):
            pl.semaphore_signal(
                barrier, inc=1, device_id={axis: lax.rem(me + d, size)}, device_id_type=MESH
            )
            greeted += 1
    pl.semaphore_wait(barrier, greeted)


def exchange(axis, size, source, target, sems):
    me = lax.axis_index(axis)
    copies = []
    for d in range(1, size):
        peer = lax.rem(me + d, size)
        copy = pltpu.make_async_remote_copy(
            src_ref=source(peer),
            dst_ref=target,
            send_sem=sems.at[0, d],
            recv_sem=sems.at[1, d],
            device_id={axis: peer},
            device_id_type=MESH,
        )
        copy.start()
        copies.append(copy)
    return copies


def attention_kernel(
    n, f, kv, group, q_ref, rk_ref, rv_ref, sk_ref, sv_ref, bias_ref, gain_ref, out_ref,
    qbuf, psend, precv, ssend, srecv, sqsend, sqrecv, hbuf,
    q_sems, p_sems, s_sems, sq_sems, h_sems, sqall=None, sqfar=None, a_sems=None,
):
    me = lax.axis_index("attn")
    mf = lax.axis_index("ffn")
    rows = q_ref.shape[1]
    req = rows // group
    scale = HEAD_DIM ** (-0.5)
    features = kv * group * HEAD_DIM * f
    if srecv.shape[0] > n:
        srecv[n:] = jnp.zeros_like(srecv[n:])
    enter((("attn", n), ("ffn", f)))
    sent = exchange("attn", n, lambda peer: q_ref, qbuf.at[me], q_sems)
    qbuf[me] = q_ref[...]
    for copy in sent:
        copy.wait()

    at_once = 4 if n % 4 == 0 else 1
    paged = sk_ref.shape[0]

    def block(b, carry):
        stats = []
        for k in range(kv):
            cols = slice(k * HEAD_DIM, (k + 1) * HEAD_DIM)
            query = qbuf[pl.ds(b * at_once, at_once), k].reshape(at_once * rows, HEAD_DIM)
            across = (((1,), (1,)), ((), ()))
            root = scale * lax.dot_general(
                query, rk_ref[:, cols], across, preferred_element_type=jnp.float32
            )
            page = scale * lax.dot_general(
                query, sk_ref[:, cols], across, preferred_element_type=jnp.float32
            )
            page = page.reshape(at_once * req, group, paged)
            page = page + bias_ref[pl.ds(b * at_once * req, at_once * req)]
            page = page.reshape(at_once * rows, paged)
            peak = jnp.maximum(
                jnp.max(root, axis=1, keepdims=True), jnp.max(page, axis=1, keepdims=True)
            )
            root = jnp.exp(root - peak)
            page = jnp.exp(page - peak)
            total = jnp.sum(root, axis=1, keepdims=True) + jnp.sum(page, axis=1, keepdims=True)
            summed = jnp.dot(
                root.astype(jnp.bfloat16), rv_ref[:, cols], preferred_element_type=jnp.float32
            ) + jnp.dot(
                page.astype(jnp.bfloat16), sv_ref[:, cols], preferred_element_type=jnp.float32
            )
            mean = (summed / total).astype(jnp.bfloat16)
            psend[pl.ds(b * at_once, at_once), k] = mean.reshape(at_once, rows, HEAD_DIM)
            stats.append(peak + jnp.log(total))
        lane = lax.broadcasted_iota(jnp.int32, (rows, 128), 1)
        for i in range(at_once):
            part = slice(i * rows, (i + 1) * rows)
            wide = jnp.broadcast_to(stats[0][part], (rows, 128))
            for k in range(1, kv):
                wide = jnp.where(lane % 8 >= k * (8 // kv), stats[k][part], wide)
            wide = jnp.concatenate([wide, jnp.zeros((128 - rows, 128), jnp.float32)], axis=0)
            ssend[b * at_once + i] = wide.T[:8]
        return carry

    lax.fori_loop(0, n // at_once, block, 0)

    sent = exchange("attn", n, lambda peer: ssend.at[peer], srecv.at[me], s_sems)
    sent += exchange("attn", n, lambda peer: psend.at[peer], precv.at[me], p_sems)
    srecv[me] = ssend[me]
    precv[me] = psend[me]
    for copy in sent:
        copy.wait()
    turned = [
        srecv[c * 16 : (c + 1) * 16].reshape(128, 128).T[:rows] for c in range(srecv.shape[0] // 16)
    ]
    attended = []
    for k in range(kv):
        def level(j):
            at = (j % 16) * 8 + k * (8 // kv)
            return turned[j // 16][:, at : at + 1]

        top = level(0)
        for j in range(1, n):
            top = jnp.maximum(top, level(j))
        total = jnp.zeros((rows, 1), jnp.float32)
        summed = jnp.zeros((rows, HEAD_DIM), jnp.float32)
        for j in range(n):
            weight = jnp.exp(level(j) - top)
            total = total + weight
            summed = summed + weight * precv[j, k].astype(jnp.float32)
        attended.append((summed / total).reshape(req, group, HEAD_DIM))
    squares = jnp.zeros((req, 1, 1), jnp.float32)
    for k in range(kv):
        lanes = jnp.sum(attended[k] * attended[k], axis=2, keepdims=True)
        squares = squares + jnp.sum(lanes, axis=1, keepdims=True)
    if sqall is not None:
        for k in range(kv):
            hidden = attended[k] * gain_ref[k].astype(jnp.float32)[None]
            hbuf[me, k] = hidden.reshape(rows, HEAD_DIM).astype(jnp.bfloat16)
        lines = [jnp.broadcast_to(squares[r], (1, 128)) for r in range(req)]
        lines.append(jnp.zeros((8 - req, 128), jnp.float32))
        sqall[me] = jnp.concatenate(lines, axis=0)
        sent = exchange("attn", n, lambda peer: sqall.at[me], sqall.at[me], a_sems)
        sent += exchange("attn", n, lambda peer: hbuf.at[me], hbuf.at[me], h_sems)
        for copy in sent:
            copy.wait()
        return exchange("ffn", f, lambda peer: sqall, sqfar.at[mf], sq_sems)
    sqsend[...] = jnp.broadcast_to(squares, sqsend.shape)
    sent = exchange("ffn", f, lambda peer: sqsend, sqrecv.at[mf], sq_sems)
    sqrecv[mf] = sqsend[...]
    for copy in sent:
        copy.wait()
    whole = sqrecv[0]
    for j in range(1, f):
        whole = whole + sqrecv[j]
    factor = lax.rsqrt(whole / features + 1e-05)[:, :1, :]
    for k in range(kv):
        hidden = attended[k] * factor * gain_ref[k].astype(jnp.float32)[None]
        hbuf[me, k] = hidden.reshape(rows, HEAD_DIM).astype(jnp.bfloat16)
    sent = exchange("attn", n, lambda peer: hbuf.at[me], hbuf.at[me], h_sems)
    for copy in sent:
        copy.wait()
    if out_ref is not None:
        out_ref[...] = hbuf[...]


def fused_kernel(
    n, f, kv, group, q_ref, rk_ref, rv_ref, sk_ref, sv_ref, bias_ref, gain_ref,
    w_ref, down_ref, out_ref,
    qbuf, psend, precv, ssend, srecv, sqsend, sqrecv, hbuf,
    q_sems, p_sems, s_sems, sq_sems, h_sems,
    ring, w_sems, lhs, acc, xsend, xrecv, active, result, osend, orecv, x_sems, o_sems,
    late_sems, sqall, sqfar, a_sems,
):
    me = lax.axis_index("attn")
    mf = lax.axis_index("ffn")
    width, _, units = w_ref.shape
    slots = ring.shape[0]
    tiles = units // 128
    steps = width // 256
    late = steps - slots
    count = acc.shape[0] // 2
    req = count // n
    pairs = w_ref.reshape(2 * width, units)

    def up_load(i):
        slot = lax.rem(i, slots)
        at = pl.ds(pl.multiple_of(i * 512, 512), 512)
        return [
            pltpu.make_async_copy(
                pairs.at[at, pl.ds(c * 128, 128)],
                ring.at[slot, pl.ds(c * 512, 512)],
                w_sems.at[slot, c],
            )
            for c in range(tiles)
        ]

    def down_load(d):
        return [
            pltpu.make_async_copy(
                down_ref.at[:, pl.ds(pl.multiple_of((4 * d + t) * 128, 128), 128)],
                ring.at[late + d, pl.ds(t * units, units)],
                w_sems.at[late + d, t],
            )
            for t in range(4)
        ]

    def first(i, carry):
        for copy in up_load(i):
            copy.start()
        return carry

    lax.fori_loop(0, slots, first, 0)
    squares_sent = attention_kernel(
        n, f, kv, group, q_ref, rk_ref, rv_ref, sk_ref, sv_ref, bias_ref, gain_ref, None,
        qbuf, psend, precv, ssend, srecv, sqsend, sqrecv, hbuf,
        q_sems, p_sems, s_sems, sq_sems, h_sems, sqall, sqfar, a_sems,
    )

    rows = count * group
    row = lax.broadcasted_iota(jnp.int32, (rows, rows), 0)
    column = lax.broadcasted_iota(jnp.int32, (rows, rows), 1)
    order = jnp.where(column == (row % count) * group + row // count, 1.0, 0.0)
    order = order.astype(jnp.bfloat16)
    feature = lax.broadcasted_iota(jnp.int32, (128, 256), 0)
    spread = lax.broadcasted_iota(jnp.int32, (128, 256), 1)
    for k in range(kv):
        held = hbuf[:, k].reshape(rows, HEAD_DIM)
        held = jnp.dot(order, held, preferred_element_type=jnp.float32).astype(jnp.bfloat16)
        halves = []
        for g in range(2):
            place = jnp.where(spread == 2 * feature + g, 1.0, 0.0).astype(jnp.bfloat16)
            half = jnp.dot(held, place, preferred_element_type=jnp.float32)
            halves.append(half.reshape(group, count, 256))
        both = jnp.concatenate(halves, axis=1).astype(jnp.bfloat16)
        lhs[k * group : (k + 1) * group] = both
    acc[...] = jnp.zeros_like(acc)

    def multiply(i):
        slot = lax.rem(i, slots)
        for copy in up_load(i):
            copy.wait()
        left = jnp.concatenate([lhs[2 * i], lhs[2 * i + 1]], axis=1)
        for c in range(0, tiles, 2):
            right = jnp.concatenate(
                [ring[slot, c * 512 : (c + 1) * 512], ring[slot, (c + 1) * 512 : (c + 2) * 512]],
                axis=1,
            )
            acc[:, c * 128 : (c + 2) * 128] += jnp.dot(
                left, right, preferred_element_type=jnp.float32
            )

    def early(i, carry):
        multiply(i)
        for copy in up_load(i + slots):
            copy.start()
        return carry

    def middle(i, carry):
        multiply(i)
        for copy in down_load(i - late):
            copy.start()
        return carry

    def final(i, carry):
        multiply(i)
        return carry

    lax.fori_loop(0, late, early, 0)
    lax.fori_loop(late, slots, middle, 0)
    lax.fori_loop(slots, steps, final, 0)

    xsend[...] = acc[...].astype(jnp.bfloat16)
    for copy in exchange("ffn", f, lambda peer: xsend, xrecv.at[mf], x_sems):
        copy.wait()
    total = acc[...]
    for d in range(1, f):
        total = total + xrecv[lax.rem(mf + d, f)].astype(jnp.float32)
    for copy in squares_sent:
        copy.wait()
    whole = sqall[...]
    for d in range(1, f):
        whole = whole + sqfar[lax.rem(mf + d, f)]
    whole = jnp.concatenate([whole[j, :req] for j in range(n)], axis=0)
    factor = lax.rsqrt(whole / (width * f) + 1e-05)[:, :1]
    gate = total[:count] * factor
    up = total[count:] * factor
    active[...] = (gate * jax.nn.sigmoid(gate) * up).astype(jnp.bfloat16)

    def columns(d, carry):
        for copy in down_load(d):
            copy.wait()
        for t in range(0, 4, 2):
            right = jnp.concatenate(
                [
                    ring[late + d, t * units : (t + 1) * units],
                    ring[late + d, (t + 1) * units : (t + 2) * units],
                ],
                axis=1,
            )
            at = pl.ds(pl.multiple_of(d * 512 + t * 128, 256), 256)
            result[:, at] = jnp.dot(active[...], right, preferred_element_type=jnp.float32)
        return carry

    middle_column = width // 2
    sent = []
    for half, sems in enumerate((o_sems, late_sems)):
        quarter = width // 1024
        lax.fori_loop(half * quarter, (half + 1) * quarter, columns, 0)
        at = slice(half * middle_column, (half + 1) * middle_column)
        for j in range(n):
            osend[half, j] = result[j * req : (j + 1) * req, at].astype(jnp.bfloat16)
        sent.append(
            exchange(
                "attn",
                n,
                lambda peer, half=half: osend.at[half, peer],
                orecv.at[half, me],
                sems,
            )
        )
    for half in range(2):
        orecv[half, me] = osend[half, me]
        for copy in sent[half]:
            copy.wait()
        mixed = orecv[half, 0].astype(jnp.float32)
        for j in range(1, n):
            mixed = mixed + orecv[half, j].astype(jnp.float32)
        at = slice(half * middle_column, (half + 1) * middle_column)
        out_ref[:, at] = mixed.astype(jnp.bfloat16)


def ffn_kernel(
    n, f, pieces, lhs_ref, w_ref, down_ref, out_ref,
    acc, held, xsend, xrecv, active, result, osend, orecv, d_sems, x_sems, o_sems,
):
    step = pl.program_id(0)
    me = lax.axis_index("attn")
    mf = lax.axis_index("ffn")
    chunk, _, units = w_ref.shape
    count = acc.shape[0] // 2
    req = count // n
    piece = held.shape[0] // pieces

    def fetch(i):
        at = pl.ds(pl.multiple_of(i * piece, piece), piece)
        return pltpu.make_async_copy(down_ref.at[at], held.at[at], d_sems.at[i])

    @pl.when(step == 0)
    def _():
        enter((("attn", n), ("ffn", f)))
        acc[...] = jnp.zeros_like(acc)

    @pl.when(step < pieces)
    def _():
        fetch(step).start()

    acc[...] += jnp.dot(
        lhs_ref[...], w_ref[...].reshape(2 * chunk, units), preferred_element_type=jnp.float32
    )

    @pl.when(step == pl.num_programs(0) - 1)
    def _():
        xsend[...] = acc[...].astype(jnp.bfloat16)
        sent = exchange("ffn", f, lambda peer: xsend, xrecv.at[mf], x_sems)
        for copy in sent:
            copy.wait()
        total = acc[...]
        for d in range(1, f):
            total = total + xrecv[lax.rem(mf + d, f)].astype(jnp.float32)
        gate = total[:count]
        active[...] = (gate * jax.nn.sigmoid(gate) * total[count:]).astype(jnp.bfloat16)

        def landed(i, carry):
            fetch(i).wait()
            return carry

        lax.fori_loop(0, pieces, landed, 0)
        width = result.shape[1]
        tile = 512 if width % 512 == 0 else width

        def columns(c, carry):
            at = pl.ds(pl.multiple_of(c * tile, tile), tile)
            result[:, at] = jnp.dot(
                active[...], held[:, at], preferred_element_type=jnp.float32
            )
            return carry

        lax.fori_loop(0, width // tile, columns, 0)
        for j in range(n):
            osend[j] = result[j * req : (j + 1) * req].astype(jnp.bfloat16)
        sent = exchange("attn", n, lambda peer: osend.at[peer], orecv.at[me], o_sems)
        orecv[me] = osend[me]
        for copy in sent:
            copy.wait()
        mixed = orecv[0].astype(jnp.float32)
        for j in range(1, n):
            mixed = mixed + orecv[j].astype(jnp.float32)
        out_ref[...] = mixed.astype(jnp.bfloat16)


def per_device(
    n, f, queries, root_keys, root_values, suffix_keys, suffix_values, suffix_lengths,
    block_table, norm_gain, w_gate_up, w_down,
):
    req = queries.shape[0]
    kv = root_keys.shape[1] // HEAD_DIM
    heads = queries.shape[1] // HEAD_DIM
    group = heads // kv
    rows = req * group
    count = req * n
    pages = suffix_keys.shape[0]
    width = heads * HEAD_DIM

    mine = lax.axis_index("attn") * pages + jnp.arange(pages, dtype=jnp.int32)
    offset = jnp.arange(MAXBLK, dtype=jnp.int32) * PAGE
    room = jnp.clip(suffix_lengths[:, None] - offset[None, :], 0, PAGE)
    matches = block_table.reshape(count, MAXBLK)[:, :, None] == mine[None, None, :]
    valid = jnp.sum(jnp.where(matches, room[:, :, None], 0), axis=1)
    alive = jnp.arange(PAGE, dtype=jnp.int32)[None, None, :] < valid[:, :, None]
    bias = jnp.where(alive, 0.0, -1e30).astype(jnp.float32).reshape(count, 1, pages * PAGE)

    blocked = queries.reshape(req, kv, group, HEAD_DIM).transpose(1, 0, 2, 3)
    blocked = blocked.reshape(kv, rows, HEAD_DIM)
    vmem = pl.BlockSpec(memory_space=pltpu.VMEM)
    share = (n, kv, rows, HEAD_DIM)

    def pair(size):
        return pltpu.SemaphoreType.DMA((2, size))

    operands = (
        blocked,
        root_keys,
        root_values,
        suffix_keys.reshape(pages * PAGE, kv * HEAD_DIM),
        suffix_values.reshape(pages * PAGE, kv * HEAD_DIM),
        bias,
        norm_gain.reshape(kv, group, HEAD_DIM),
    )
    scratch = [
        pltpu.VMEM(share, jnp.bfloat16),
        pltpu.VMEM(share, jnp.bfloat16),
        pltpu.VMEM(share, jnp.bfloat16),
        pltpu.VMEM((n, 8, 128), jnp.float32),
        pltpu.VMEM(((n + 15) // 16 * 16, 8, 128), jnp.float32),
        pltpu.VMEM((req, 8, 128), jnp.float32),
        pltpu.VMEM((f, req, 8, 128), jnp.float32),
        pltpu.VMEM(share, jnp.bfloat16),
        pair(n),
        pair(n),
        pair(n),
        pair(f),
        pair(n),
    ]
    units = w_gate_up.shape[2]
    if units % 256 == 0 and width % 2048 == 0 and count % 8 == 0 and req < 8:
        slots = width // 256 * 3 // 4
        return pl.pallas_call(
            functools.partial(fused_kernel, n, f, kv, group),
            out_shape=jax.ShapeDtypeStruct((req, width), jnp.bfloat16),
            in_specs=[vmem] * 7 + [pl.BlockSpec(memory_space=pl.ANY)] * 2,
            out_specs=vmem,
            scratch_shapes=scratch
            + [
                pltpu.VMEM((slots, 4 * units, 128), jnp.bfloat16),
                pltpu.SemaphoreType.DMA((slots, units // 128)),
                pltpu.VMEM((heads, 2 * count, 256), jnp.bfloat16),
                pltpu.VMEM((2 * count, units), jnp.float32),
                pltpu.VMEM((2 * count, units), jnp.bfloat16),
                pltpu.VMEM((f, 2 * count, units), jnp.bfloat16),
                pltpu.VMEM((count, units), jnp.bfloat16),
                pltpu.VMEM((count, width), jnp.float32),
                pltpu.VMEM((2, n, req, width // 2), jnp.bfloat16),
                pltpu.VMEM((2, n, req, width // 2), jnp.bfloat16),
                pair(f),
                pair(n),
                pair(n),
                pltpu.VMEM((n, 8, 128), jnp.float32),
                pltpu.VMEM((f, n, 8, 128), jnp.float32),
                pair(n),
            ],
            compiler_params=pltpu.CompilerParams(
                collective_id=2, has_side_effects=True, vmem_limit_bytes=58 << 20
            ),
        )(*operands, w_gate_up, w_down)
    hidden = pl.pallas_call(
        functools.partial(attention_kernel, n, f, kv, group),
        out_shape=jax.ShapeDtypeStruct(share, jnp.bfloat16),
        in_specs=[vmem] * 7,
        out_specs=vmem,
        scratch_shapes=scratch,
        compiler_params=pltpu.CompilerParams(
            collective_id=0, has_side_effects=True, vmem_limit_bytes=40 << 20
        ),
    )(*operands)
    hidden = hidden.reshape(n, kv, req, group, HEAD_DIM).transpose(0, 2, 1, 3, 4)
    hidden = hidden.reshape(count, width)
    blank = jnp.zeros_like(hidden)
    lhs = jnp.concatenate(
        [
            jnp.stack([hidden, blank], axis=-1).reshape(count, 2 * width),
            jnp.stack([blank, hidden], axis=-1).reshape(count, 2 * width),
        ],
        axis=0,
    )

    chunk = 128
    steps = width // chunk
    pieces = 1
    for p in range(1, steps + 1):
        if units % (16 * p) == 0:
            pieces = p
    return pl.pallas_call(
        functools.partial(ffn_kernel, n, f, pieces),
        grid=(steps,),
        out_shape=jax.ShapeDtypeStruct((req, width), jnp.bfloat16),
        in_specs=[
            pl.BlockSpec((2 * count, 2 * chunk), lambda i: (0, i)),
            pl.BlockSpec((chunk, 2, units), lambda i: (i, 0, 0)),
            pl.BlockSpec(memory_space=pl.ANY),
        ],
        out_specs=pl.BlockSpec((req, width), lambda i: (0, 0)),
        scratch_shapes=[
            pltpu.VMEM((2 * count, units), jnp.float32),
            pltpu.VMEM((units, width), jnp.bfloat16),
            pltpu.VMEM((2 * count, units), jnp.bfloat16),
            pltpu.VMEM((f, 2 * count, units), jnp.bfloat16),
            pltpu.VMEM((count, units), jnp.bfloat16),
            pltpu.VMEM((count, width), jnp.float32),
            pltpu.VMEM((n, req, width), jnp.bfloat16),
            pltpu.VMEM((n, req, width), jnp.bfloat16),
            pltpu.SemaphoreType.DMA((pieces,)),
            pair(f),
            pair(n),
        ],
        compiler_params=pltpu.CompilerParams(
            collective_id=1, has_side_effects=True, vmem_limit_bytes=52 << 20
        ),
    )(lhs, w_gate_up, w_down)


def solution(mesh):
    return jax.shard_map(
        functools.partial(per_device, mesh.shape["attn"], mesh.shape["ffn"]),
        mesh=mesh,
        in_specs=(
            P(("groups", "attn"), "ffn"),
            P(("groups", "attn"), "ffn"),
            P(("groups", "attn"), "ffn"),
            P(("groups", "attn"), None, "ffn"),
            P(("groups", "attn"), None, "ffn"),
            P("groups"),
            P("groups"),
            P("ffn"),
            P("ffn", None, "attn"),
            P("attn", "ffn"),
        ),
        out_specs=P(("groups", "attn"), "ffn"),
        check_vma=False,
    )
```
